256 devices in a mesh: img: 8 (over z_hi, core), txt: 32 (over y, x, z_lo).
Axes of the slice: x: 4, y: 4, z: 8 (z_hi: 4, z_lo: 2; z = z_hi * 2 + z_lo), core: 2. Of those that a mesh axis runs over, the one named last changes fastest.
Arguments:
- image_emb: float32 [8192, 1152], P(('img', 'txt')), may hold values from -6 to 6
- text_emb: float32 [8192, 1152], P(('img', 'txt')), may hold values from -6 to 6
- logit_scale: float32 [1], replicated, may hold values from 8 to 12
- logit_bias: float32 [1], replicated, may hold values from -4 to -2
Outputs:
- loss: float32 [1], replicated
- image_grad: float32 [8192, 1152], P(('img', 'txt'))
- text_grad: float32 [8192, 1152], P(('img', 'txt'))
The draws below stay inside these ranges and needn't reach their ends.
All inputs are finite; a program needn't handle non-finite values.
Results may differ from the reference program's by a relative error of at most 0.0003.
Values sent between devices are 32-bit elements; how exact they have to be, the bound alone decides.
No kernel may reach another device: no remote copies, remote signals or barrier semaphores. Data moves between devices by JAX's collectives and lax.ppermute only.
A program may use at most 64 MiB of HBM per device.

```python
import math
import jax
import jax.numpy as jnp
from jax import lax

D = 1152
BATCH = 8192


def steps_of(key, shape, cuts, smallest, largest):
    gain, own = 1.0, jax.random.fold_in(key, 6)
    for axis_at, blocks in cuts:
        steps = jnp.exp(jax.random.uniform(jax.random.fold_in(own, axis_at), (blocks,), jnp.float32, smallest / len(cuts), largest / len(cuts)))
        gain = gain * jnp.repeat(steps, shape[axis_at] // blocks).reshape([-1 if axis == axis_at else 1 for axis in range(len(shape))])
    return gain


def gaussian(rng, extent, width, most, split=(), held_as=jnp.bfloat16):
    values = width * jax.random.normal(rng, extent, jnp.float32)
    if split:
        values = values * steps_of(rng, extent, split, -0.22, 0.18)
    return jnp.clip(values, -most, most).astype(held_as)


def setup_inputs(seed: int = 0) -> dict:
    key_of = jax.random.split(jax.random.key(seed), 5)
    return {
        "image_emb": gaussian(key_of[0], (BATCH, D), 1.0, 6.0, ((0, 256),), jnp.float32),
        "text_emb": gaussian(key_of[1], (BATCH, D), 1.0, 6.0, ((0, 256),), jnp.float32),
        "logit_scale": jnp.clip(jax.random.uniform(key_of[2], (1,), jnp.float32, 8.0, 12.0), 8.0, 12.0),
        "logit_bias": jnp.clip(jax.random.uniform(key_of[3], (1,), jnp.float32, -4.0, -2.0), -4.0, -2.0),
    }


def normalize(embed):
    inverse = lax.rsqrt(lax.optimization_barrier(jnp.sum(embed * embed, axis=1, keepdims=True)) + 1e-06)
    return (embed * inverse, inverse)

def reference(image_emb, text_emb, logit_scale, logit_bias):
    image_unit, image_inv = normalize(image_emb)
    text_unit, text_inv = normalize(text_emb)
    temper = logit_scale[0]
    offset = logit_bias[0]
    block = math.gcd(BATCH, 1024)
    columns = jnp.arange(BATCH, dtype=jnp.int32)

    def one_block(carry, index):
        text_acc, total = carry
        start = (index * block).astype(jnp.int32)
        rows = lax.dynamic_slice_in_dim(image_unit, start, block, 0)
        logits = temper * jnp.dot(rows, text_unit.T, precision=lax.Precision.HIGHEST) + offset
        row_ids = start + jnp.arange(block, dtype=jnp.int32)
        label = jnp.where(row_ids[:, None] == columns[None, :], 1.0, -1.0).astype(logits.dtype)
        total = total + jnp.sum(jax.nn.softplus(-label * logits))
        coef = -label * jax.nn.sigmoid(-label * logits)
        image_part = temper * jnp.dot(coef, text_unit, precision=lax.Precision.HIGHEST)
        text_acc = text_acc + temper * jnp.dot(coef.T, rows, precision=lax.Precision.HIGHEST)
        return ((text_acc, total), image_part)
    start_carry = (jnp.zeros_like(text_unit), jnp.zeros((), image_unit.dtype))
    (text_unit_grad, total), parts = lax.scan(one_block, start_carry, jnp.arange(BATCH // block, dtype=jnp.int32))
    image_unit_grad = parts.reshape(BATCH, image_unit.shape[1])
    image_grad = (image_unit_grad - image_unit * lax.optimization_barrier(jnp.sum(image_unit * image_unit_grad, axis=1, keepdims=True))) * image_inv
    text_grad = (text_unit_grad - text_unit * lax.optimization_barrier(jnp.sum(text_unit * text_unit_grad, axis=1, keepdims=True))) * text_inv
    loss = (total / BATCH).reshape(1)
    return (loss, image_grad, text_grad)
```

```python
import itertools
import jax
import jax.numpy as jnp
from jax import lax
from jax.sharding import PartitionSpec as P

AXES = ("img", "txt")
NX, NY, NZ = 4, 4, 8
HIGH = lax.Precision.HIGH


def place(z, y, x, core):
    return ((z // 2) * 2 + core) * 32 + (y * NX + x) * 2 + z % 2


def pairs(target):
    out = []
    for z, y, x, core in itertools.product(range(NZ), range(NY), range(NX), range(2)):
        tz, ty, tx, tc = target(z, y, x, core)
        out.append((place(z, y, x, core), place(tz % NZ, ty % NY, tx % NX, tc)))
    return out


def send(value, target):
    return lax.ppermute(value, AXES, pairs(target))


def swap(value):
    return send(value, lambda z, y, x, core: (z, y, x, 1 - core))


def first(value, d):
    return send(value, lambda z, y, x, core: (z, y, x + d, core) if core == 0 else (z, y + d, x, core))


def second(value, d):
    return send(value, lambda z, y, x, core: (z, y + d, x, core) if core == 0 else (z, y, x + d, core))


def along_z(value, d):
    return send(value, lambda z, y, x, core: (z + d if core == 0 else z - d, y, x, core))


STEPS = (1, 3, 2)


def normalize(embed):
    inverse = lax.rsqrt(jnp.sum(embed * embed, axis=1, keepdims=True) + 1e-06)
    return (embed * inverse, inverse)


def gather_image(block):
    four = jnp.concatenate([block] + [first(block, d) for d in STEPS])
    return jnp.concatenate([four] + [second(four, d) for d in STEPS])


def gather_text(block):
    pair = jnp.concatenate([block, swap(block)])
    chain = []
    held = pair
    for step in range(4):
        held = along_z(held if step < 3 else held[: block.shape[0]], 1)
        chain.append(held)
    chain = jnp.concatenate(chain)
    return jnp.concatenate([pair, chain, swap(chain)])


def scatter_image(part, rows):
    four = [part[4 * rows * i : 4 * rows * (i + 1)] for i in range(4)]
    got = [second(four[i + 1], -d) for i, d in enumerate(STEPS)]
    total = four[0] + got[0] + got[1] + got[2]
    one = [total[rows * i : rows * (i + 1)] for i in range(4)]
    got = [first(one[i + 1], -d) for i, d in enumerate(STEPS)]
    return one[0] + got[0] + got[1] + got[2]


def scatter_text(part, rows):
    other = swap(jnp.concatenate([part[rows : 2 * rows], part[9 * rows :]]))
    own = part[:rows] + other[:rows]
    chain = part[2 * rows : 9 * rows] + other[rows:]
    held = along_z(chain[6 * rows :], -1)
    held = along_z(chain[4 * rows : 6 * rows] + jnp.concatenate([held, jnp.zeros_like(held)]), -1)
    held = along_z(chain[2 * rows : 4 * rows] + held, -1)
    held = along_z(chain[: 2 * rows] + held, -1)
    return own + held[:rows] + swap(held[rows:])


def sum_all(value):
    value = value + swap(value)
    for bit in (1, 2):
        value = value + send(value, lambda z, y, x, core: (z, y, x ^ bit, core))
        value = value + send(value, lambda z, y, x, core: (z, y ^ bit, x, core))
    for bit in (1, 2, 4):
        value = value + send(value, lambda z, y, x, core: (z ^ bit, y, x, core))
    return value


def on_device(image_emb, text_emb, logit_scale, logit_bias):
    rows = image_emb.shape[0]
    image_unit, image_inv = normalize(image_emb)
    text_unit, text_inv = normalize(text_emb)
    temper = logit_scale[0]
    offset = logit_bias[0]
    texts = gather_text(text_unit)
    images = gather_image(image_unit)

    logits = temper * jnp.dot(images, texts.T, precision=HIGH) + offset
    row = lax.broadcasted_iota(jnp.int32, logits.shape, 0)
    col = lax.broadcasted_iota(jnp.int32, logits.shape, 1)
    label = jnp.where((row == col) & (row < rows), 1.0, -1.0).astype(jnp.float32)
    total = jnp.sum(jax.nn.softplus(-label * logits))
    coef = -label * jax.nn.sigmoid(-label * logits)
    image_part = temper * jnp.dot(coef, texts, precision=HIGH)
    text_part = temper * jnp.dot(coef.T, images, precision=HIGH)

    text_unit_grad = scatter_text(text_part, rows)
    image_unit_grad = scatter_image(image_part, rows)
    loss = (sum_all(total.reshape(1)) / (rows * 2 * NX * NY * NZ)).reshape(1)
    image_grad = (
        image_unit_grad - image_unit * jnp.sum(image_unit * image_unit_grad, axis=1, keepdims=True)
    ) * image_inv
    text_grad = (
        text_unit_grad - text_unit * jnp.sum(text_unit * text_unit_grad, axis=1, keepdims=True)
    ) * text_inv
    return (loss, image_grad, text_grad)


def solution(mesh):
    return jax.shard_map(
        on_device,
        mesh=mesh,
        in_specs=(P(("img", "txt"), None), P(("img", "txt"), None), P(), P()),
        out_specs=(P(), P(("img", "txt"), None), P(("img", "txt"), None)),
        check_vma=False,
    )
```

```python
import functools
import itertools
import jax
import jax.numpy as jnp
from jax import lax
from jax.experimental import pallas as pl
from jax.experimental.pallas import tpu as pltpu
from jax.sharding import PartitionSpec as P

AXES = ("img", "txt")
NX, NY, NZ = 4, 4, 8


def place(z, y, x, core):
    return ((z // 2) * 2 + core) * 32 + (y * NX + x) * 2 + z % 2


def pairs(target):
    out = []
    for z, y, x, core in itertools.product(range(NZ), range(NY), range(NX), range(2)):
        tz, ty, tx, tc = target(z, y, x, core)
        out.append((place(z, y, x, core), place(tz % NZ, ty % NY, tx % NX, tc)))
    return out


def send(value, target):
    return lax.ppermute(value, AXES, pairs(target))


def swap(value):
    return send(value, lambda z, y, x, core: (z, y, x, 1 - core))


def first(value, d):
    return send(value, lambda z, y, x, core: (z, y, x + d, core) if core == 0 else (z, y + d, x, core))


def second(value, d):
    return send(value, lambda z, y, x, core: (z, y + d, x, core) if core == 0 else (z, y, x + d, core))


def along_z(value, d):
    return send(value, lambda z, y, x, core: (z + d if core == 0 else z - d, y, x, core))


STEPS = (1, 3, 2)
SHEETS = [
    [place(z, k, x, 0) for z in range(NZ) for x in range(NX)] + [place(z, y, k, 1) for z in range(NZ) for y in range(NY)]
    for k in range(NX)
]


def after(values, *others):
    return lax.optimization_barrier((values, others))[0]


NT = (((1,), (1,)), ((), ()))
TN = (((0,), (0,)), ((), ()))
NN = (((1,), (0,)), ((), ()))
VMEM = pl.BlockSpec(memory_space=pltpu.VMEM)
SMEM = pl.BlockSpec(memory_space=pltpu.SMEM)
GRANT = pltpu.CompilerParams(vmem_limit_bytes=40 << 20)


def f32(*shape):
    return jax.ShapeDtypeStruct(shape, jnp.float32)


def b16(*shape):
    return jax.ShapeDtypeStruct(shape, jnp.bfloat16)


def halves(value):
    high = value.astype(jnp.bfloat16)
    return high, (value - high.astype(jnp.float32)).astype(jnp.bfloat16)


def dot3(a, b, dims):
    dot = functools.partial(lax.dot_general, dimension_numbers=dims, preferred_element_type=jnp.float32)
    return dot(a[0], b[0]) + (dot(a[0], b[1]) + dot(a[1], b[0]))


def unit_halves(refs, high, low):
    at = 0
    for ref in refs:
        rows = ref.shape[0]
        raw = ref[...]
        unit = raw * lax.rsqrt(jnp.sum(raw * raw, axis=1, keepdims=True) + 1e-06)
        high[at : at + rows, :], low[at : at + rows, :] = halves(unit)
        at += rows


def pair_terms(logits, own):
    if own:
        row = lax.broadcasted_iota(jnp.int32, logits.shape, 0)
        col = lax.broadcasted_iota(jnp.int32, logits.shape, 1)
        same = (row == col) & (row < own)
        logits = jnp.where(same, -logits, logits)
    small = jnp.exp(-jnp.abs(logits))
    loss = jnp.sum(jnp.maximum(logits, 0.0) + jnp.log1p(small))
    part = 1.0 / (1.0 + small)
    coef = jnp.where(logits >= 0, part, small * part)
    if own:
        coef = jnp.where(same, -coef, coef)
    return loss, coef


def near_kernel(own, scale, bias, *refs):
    i_refs, t_refs = refs[:4], refs[4:9]
    image_part, pay, own_part, one_part, two_part, ihi, ilo, loss, thi, tlo = refs[9:]
    unit_halves(i_refs, ihi, ilo)
    unit_halves(t_refs, thi, tlo)
    images = ihi[...], ilo[...]
    texts = thi[...], tlo[...]
    logits = scale[0] * dot3(images, texts, NT) + bias[0]
    total, coef = pair_terms(logits, own)
    loss[...] = jnp.full(loss.shape, total, jnp.float32)
    coef = halves(coef * scale[0])
    text_part = dot3(coef, images, TN)
    own_part[...] = text_part[:own]
    one_part[...] = text_part[2 * own : 4 * own]
    two_part[...] = text_part[4 * own : 6 * own]
    pay[: 4 * own, :] = text_part[6 * own :]
    pay[4 * own :, :] = text_part[own : 2 * own]
    image_part[...] = dot3(coef, texts, NN)


def far_kernel(scale, bias, ihi, ilo, loss_in, t0, t1, pay, rest, chi, clo, thi, tlo, loss):
    unit_halves((t0, t1), thi, tlo)
    images = ihi[...], ilo[...]
    texts = thi[...], tlo[...]
    logits = scale[0] * dot3(images, texts, NT) + bias[0]
    total, coef = pair_terms(logits, 0)
    loss[...] = loss_in[...] + total
    coef = halves(coef * scale[0])
    chi[...], clo[...] = coef
    text_part = dot3(coef, images, TN)
    count = t0.shape[0]
    rest[...] = text_part[:count]
    pay[...] = text_part[count:]


def last_kernel(chi, clo, thi, tlo, image_in, loss, out0, out1, out2, out3):
    part = dot3((chi[...], clo[...]), (thi[...], tlo[...]), NN) + image_in[...]
    rows = part.shape[0] // 4
    note = jnp.broadcast_to(loss[:, :1], (8, part.shape[1]))
    for k, out in enumerate((out0, out1, out2, out3)):
        out[:rows, :] = part[rows * k : rows * (k + 1)]
        out[rows:, :] = note


def sum_kernel(in0, in1, in2, in3, out0, out1, out2, out3, note):
    total = (in0[...] + in3[...]) + (in1[...] + in2[...])
    rows = (total.shape[0] - 8) // 4
    for k, out in enumerate((out0, out1, out2, out3)):
        out[...] = total[rows * k : rows * (k + 1)]
    note[...] = total[4 * rows :, :128]


def near_call(scale, bias, images, texts):
    own, width = texts[0].shape
    rows, cols = 16 * own, 10 * own
    return pl.pallas_call(
        functools.partial(near_kernel, own),
        out_shape=[f32(rows, width), f32(5 * own, width), f32(own, width), f32(2 * own, width), f32(2 * own, width)]
        + [b16(rows, width), b16(rows, width), f32(8, 128)],
        in_specs=[SMEM, SMEM] + [VMEM] * 9,
        out_specs=[VMEM] * 8,
        scratch_shapes=[pltpu.VMEM((cols, width), jnp.bfloat16)] * 2,
        cost_estimate=pl.CostEstimate(
            flops=18 * rows * cols * width, bytes_accessed=12 * rows * width, transcendentals=rows * cols
        ),
        compiler_params=GRANT,
    )(scale, bias, *images, *texts)


def far_call(scale, bias, ihi, ilo, loss, t0, t1):
    count = t0.shape[0]
    rows, width = ihi.shape
    return pl.pallas_call(
        far_kernel,
        out_shape=[f32(count, width), f32(count, width), b16(rows, 2 * count), b16(rows, 2 * count)]
        + [b16(2 * count, width), b16(2 * count, width), f32(8, 128)],
        in_specs=[SMEM, SMEM] + [VMEM] * 5,
        out_specs=[VMEM] * 7,
        cost_estimate=pl.CostEstimate(
            flops=24 * rows * count * width, bytes_accessed=8 * rows * width, transcendentals=2 * rows * count
        ),
        compiler_params=GRANT,
    )(scale, bias, ihi, ilo, loss, t0, t1)


def last_call(chi, clo, thi, tlo, image_part, loss):
    rows, width = image_part.shape
    return pl.pallas_call(
        last_kernel,
        out_shape=[f32(rows // 4 + 8, width)] * 4,
        in_specs=[VMEM] * 6,
        out_specs=[VMEM] * 4,
        cost_estimate=pl.CostEstimate(
            flops=6 * rows * chi.shape[1] * width, bytes_accessed=8 * rows * width, transcendentals=0
        ),
        compiler_params=GRANT,
    )(chi, clo, thi, tlo, image_part, loss)


def sum_call(parts):
    rows, width = parts[0].shape
    return pl.pallas_call(
        sum_kernel,
        out_shape=[f32((rows - 8) // 4, width)] * 4 + [f32(8, 128)],
        in_specs=[VMEM] * 4,
        out_specs=[VMEM] * 5,
        compiler_params=GRANT,
    )(*parts)


def normalize(embed):
    inverse = lax.rsqrt(jnp.sum(embed * embed, axis=1, keepdims=True) + 1e-06)
    return (embed * inverse, inverse)


def on_device(image_emb, text_emb, logit_scale, logit_bias):
    rows = image_emb.shape[0]
    other = swap(text_emb)
    four = [first(image_emb, d) for d in STEPS]
    pair = jnp.concatenate([text_emb, other])
    one = along_z(pair, 1)
    two = along_z(pair, 2)
    four = jnp.concatenate([image_emb] + four)
    images = [four] + [second(four, d) for d in STEPS]
    far = along_z(jnp.concatenate([one, two[:rows]]), 2)
    near_swap = swap(jnp.concatenate([one, two]))

    image_part, near_pay, own_part, one_part, two_part, ihi, ilo, loss = near_call(
        logit_scale, logit_bias, images, [text_emb, other, one, two, near_swap]
    )
    far = after(far, loss)
    far_swap = swap(far)
    near_back = swap(near_pay)
    far_pay, far_part, chi, clo, thi, tlo, loss = far_call(
        logit_scale, logit_bias, after(ihi, near_back), ilo, loss, far, far_swap
    )
    far_pay = swap(far_pay)
    four = last_call(chi, clo, thi, tlo, image_part, loss)
    far_pay = after(far_part + far_pay, four)
    back = along_z(far_pay, -2)
    four = after(four, far_pay)
    got = [second(four[i + 1], -d) for i, d in enumerate(STEPS)]
    one_part = one_part + near_back[: 2 * rows] + back[: 2 * rows]
    two_part = two_part + near_back[2 * rows : 4 * rows]
    two_part = jnp.concatenate([two_part[:rows] + back[2 * rows :], two_part[rows:]])
    back = along_z(one_part, -1) + along_z(two_part, -2)
    *four, note = sum_call([four[0]] + got)
    got = [first(four[i + 1], -d) for i, d in enumerate(STEPS)]
    notes = jnp.broadcast_to(note[:1, :128].reshape(1, 1, 128), (64, 1, 128))
    notes = lax.all_to_all(notes, AXES, 0, 0, axis_index_groups=SHEETS, tiled=True)
    loss = (jnp.sum(notes[:, 0, 0]) / (rows * 2 * NX * NY * NZ)).reshape(1)
    total = (four[0] + got[2]) + (got[0] + got[1])
    text_unit_grad = own_part + near_back[4 * rows :] + back[:rows] + swap(back[rows:])
    image_unit_grad = total

    image_unit, image_inv = normalize(image_emb)
    text_unit, text_inv = normalize(text_emb)
    image_grad = (
        image_unit_grad - image_unit * jnp.sum(image_unit * image_unit_grad, axis=1, keepdims=True)
    ) * image_inv
    text_grad = (
        text_unit_grad - text_unit * jnp.sum(text_unit * text_unit_grad, axis=1, keepdims=True)
    ) * text_inv
    return (loss, image_grad, text_grad)


def solution(mesh):
    return jax.shard_map(
        on_device,
        mesh=mesh,
        in_specs=(P(("img", "txt"), None), P(("img", "txt"), None), P(), P()),
        out_specs=(P(), P(("img", "txt"), None), P(("img", "txt"), None)),
        check_vma=False,
    )
```

```python
import functools
import itertools
import jax
import jax.numpy as jnp
from jax import lax
from jax.experimental import pallas as pl
from jax.experimental.pallas import tpu as pltpu
from jax.sharding import PartitionSpec as P

AXES = ("img", "txt")
NX, NY, NZ = 4, 4, 8


def place(z, y, x, core):
    return ((z // 2) * 2 + core) * 32 + (y * NX + x) * 2 + z % 2


def pairs(target):
    out = []
    for z, y, x, core in itertools.product(range(NZ), range(NY), range(NX), range(2)):
        tz, ty, tx, tc = target(z, y, x, core)
        out.append((place(z, y, x, core), place(tz % NZ, ty % NY, tx % NX, tc)))
    return out


def send(value, target):
    return lax.ppermute(value, AXES, pairs(target))


def swap(value):
    return send(value, lambda z, y, x, core: (z, y, x, 1 - core))


def first(value, d):
    return send(value, lambda z, y, x, core: (z, y, x + d, core) if core == 0 else (z, y + d, x, core))


def second(value, d):
    return send(value, lambda z, y, x, core: (z, y + d, x, core) if core == 0 else (z, y, x + d, core))


def along_z(value, d):
    return send(value, lambda z, y, x, core: (z + d if core == 0 else z - d, y, x, core))


STEPS = (1, 3, 2)

def add_from(value, target):
    return value + send(value, target)


def after(values, *others):
    return lax.optimization_barrier((values, others))[0]


NT = (((1,), (1,)), ((), ()))
TN = (((0,), (0,)), ((), ()))
NN = (((1,), (0,)), ((), ()))
VMEM = pl.BlockSpec(memory_space=pltpu.VMEM)
SMEM = pl.BlockSpec(memory_space=pltpu.SMEM)
GRANT = pltpu.CompilerParams(vmem_limit_bytes=40 << 20)


def f32(*shape):
    return jax.ShapeDtypeStruct(shape, jnp.float32)


def b16(*shape):
    return jax.ShapeDtypeStruct(shape, jnp.bfloat16)


def halves(value):
    high = value.astype(jnp.bfloat16)
    return high, (value - high.astype(jnp.float32)).astype(jnp.bfloat16)


def dot3(a, b, dims):
    dot = functools.partial(lax.dot_general, dimension_numbers=dims, preferred_element_type=jnp.float32)
    return dot(a[0], b[0]) + (dot(a[0], b[1]) + dot(a[1], b[0]))


def unit_halves(refs, high, low):
    at = 0
    for ref in refs:
        rows = ref.shape[0]
        raw = ref[...]
        unit = raw * lax.rsqrt(jnp.sum(raw * raw, axis=1, keepdims=True) + 1e-06)
        high[at : at + rows, :], low[at : at + rows, :] = halves(unit)
        at += rows


def pair_terms(logits, own):
    if own:
        row = lax.broadcasted_iota(jnp.int32, logits.shape, 0)
        col = lax.broadcasted_iota(jnp.int32, logits.shape, 1)
        same = (row == col) & (row < own)
        logits = jnp.where(same, -logits, logits)
    small = jnp.exp(-jnp.abs(logits))
    loss = jnp.sum(jnp.maximum(logits, 0.0) + jnp.log1p(small))
    part = 1.0 / (1.0 + small)
    coef = jnp.where(logits >= 0, part, small * part)
    if own:
        coef = jnp.where(same, -coef, coef)
    return loss, coef


def two_parts(total):
    coarse = jnp.round(total * (1.0 / 128.0)) * 128.0
    fine = jnp.round((total - coarse) * 512.0) * (1.0 / 512.0)
    return jnp.where(lax.broadcasted_iota(jnp.int32, (8, 128), 1) < 64, coarse, fine)


def group_kernel(own, count, scale, bias, *refs):
    raws = refs[:count]
    if own:
        texts = refs[count : count + 4]
        image_part, ihi, ilo, text_part, loss, thi, tlo = refs[count + 4 :]
        unit_halves(texts, thi, tlo)
    else:
        thi, tlo, text_in, loss_in, image_part, ihi, ilo, text_part, loss = refs[count:]
    unit_halves(raws, ihi, ilo)
    images = ihi[...], ilo[...]
    texts = thi[...], tlo[...]
    logits = scale[0] * dot3(images, texts, NT) + bias[0]
    total, coef = pair_terms(logits, own)
    coef = halves(coef * scale[0])
    image_part[...] = dot3(coef, texts, NN)
    part = dot3(coef, images, TN)
    if own:
        text_part[...] = part
        loss[...] = jnp.full(loss.shape, total, jnp.float32)
    else:
        text_part[...] = text_in[...] + part
        loss[...] = loss_in[...] + total


def mid_kernel(scale, bias, h0, l0, h1, l1, loss_in, raw, ihi, ilo, part, chi, clo, thi, tlo, loss):
    rows = h0.shape[0]
    ihi[:rows, :], ilo[:rows, :] = h0[...], l0[...]
    ihi[rows:, :], ilo[rows:, :] = h1[...], l1[...]
    unit_halves((raw,), thi, tlo)
    images = ihi[...], ilo[...]
    logits = scale[0] * dot3(images, (thi[...], tlo[...]), NT) + bias[0]
    total, coef = pair_terms(logits, 0)
    loss[...] = loss_in[...] + total
    coef = halves(coef * scale[0])
    chi[...], clo[...] = coef
    part[...] = dot3(coef, images, TN)


def far_kernel(scale, bias, ihi, ilo, loss_in, raw, chi, clo, thi, tlo, loss):
    unit_halves((raw,), thi, tlo)
    logits = scale[0] * dot3((ihi[...], ilo[...]), (thi[...], tlo[...]), NT) + bias[0]
    total, coef = pair_terms(logits, 0)
    loss[...] = two_parts(loss_in[...] + total)
    chi[...], clo[...] = halves(coef * scale[0])


def last_kernel(ihi, ilo, mhi, mlo, uhi, ulo, chi, clo, thi, tlo, in0, in1, other, pay, *outs):
    coef = chi[...], clo[...]
    count = thi.shape[0]
    pay[:count, :] = dot3(coef, (ihi[...], ilo[...]), TN)
    pay[count:, :] = other[...]
    part = dot3((mhi[...], mlo[...]), (uhi[...], ulo[...]), NN) + dot3(coef, (thi[...], tlo[...]), NN)
    rows = in0.shape[0]
    outs[0][...] = in0[...] + part[:rows]
    for k, out in enumerate(outs[1:]):
        out[...] = in1[rows * k : rows * (k + 1), :] + part[rows * (k + 1) : rows * (k + 2)]


def sum_kernel(in0, in1, in2, in3, out0, out1, out2, out3):
    total = (in0[...] + in3[...]) + (in1[...] + in2[...])
    rows = (total.shape[0] - 8) // 4
    for k, out in enumerate((out0, out1, out2, out3)):
        out[:rows, :] = total[rows * k : rows * (k + 1)]
        out[rows:, :] = total[4 * rows :]


def cost(rows, cols, width, dots):
    return pl.CostEstimate(flops=6 * dots * rows * cols * width, bytes_accessed=4 * rows * width, transcendentals=0)


def group_call(scale, bias, raws, texts, start=None):
    width = raws[0].shape[1]
    rows = sum(raw.shape[0] for raw in raws)
    cols = sum(text.shape[0] for text in texts) if start is None else texts[0].shape[0]
    operands = [scale, bias, *raws, *texts, *(start or ())]
    shapes = [f32(rows, width), b16(rows, width), b16(rows, width), f32(cols, width), f32(8, 128)]
    if start is None:
        shapes += [b16(cols, width)] * 2
    return pl.pallas_call(
        functools.partial(group_kernel, texts[0].shape[0] if start is None else 0, len(raws)),
        out_shape=shapes,
        in_specs=[SMEM, SMEM] + [VMEM] * (len(operands) - 2),
        out_specs=[VMEM] * len(shapes),
        cost_estimate=cost(rows, cols, width, 3),
        compiler_params=GRANT,
    )(*operands)


def mid_call(scale, bias, images, loss, raw):
    count, width = raw.shape
    rows = images[0].shape[0] + images[2].shape[0]
    return pl.pallas_call(
        mid_kernel,
        out_shape=[b16(rows, width)] * 2
        + [f32(count, width)]
        + [b16(rows, count)] * 2
        + [b16(count, width)] * 2
        + [f32(8, 128)],
        in_specs=[SMEM, SMEM] + [VMEM] * 6,
        out_specs=[VMEM] * 8,
        cost_estimate=cost(rows, count, width, 2),
        compiler_params=GRANT,
    )(scale, bias, *images, loss, raw)


def far_call(scale, bias, ihi, ilo, loss, raw):
    count, width = raw.shape
    rows = ihi.shape[0]
    return pl.pallas_call(
        far_kernel,
        out_shape=[b16(rows, count)] * 2 + [b16(count, width)] * 2 + [f32(8, 128)],
        in_specs=[SMEM, SMEM] + [VMEM] * 4,
        out_specs=[VMEM] * 5,
        cost_estimate=cost(rows, count, width, 1),
        compiler_params=GRANT,
    )(scale, bias, ihi, ilo, loss, raw)


def last_call(images, mid, far, starts, other):
    rows, width = images[0].shape
    count = far[0].shape[1]
    return pl.pallas_call(
        last_kernel,
        out_shape=[f32(count + other.shape[0], width)] + [f32(rows // 4, width)] * 4,
        in_specs=[VMEM] * 13,
        out_specs=[VMEM] * 5,
        cost_estimate=cost(rows, count, width, 5),
        compiler_params=GRANT,
    )(*images, *mid, *far, *starts, other)


def sum_call(parts):
    rows, width = parts[0].shape
    return pl.pallas_call(
        sum_kernel,
        out_shape=[f32((rows - 8) // 4 + 8, width)] * 4,
        in_specs=[VMEM] * 4,
        out_specs=[VMEM] * 4,
        compiler_params=GRANT,
    )(*parts)


def normalize(embed):
    inverse = lax.rsqrt(jnp.sum(embed * embed, axis=1, keepdims=True) + 1e-06)
    return (embed * inverse, inverse)


def on_device(image_emb, text_emb, logit_scale, logit_bias):
    rows = image_emb.shape[0]
    other = swap(text_emb)
    four = [first(image_emb, d) for d in STEPS]
    pair = jnp.concatenate([text_emb, other])
    one = along_z(pair, 1)
    two = along_z(pair, 2)
    four = jnp.concatenate([image_emb] + four)
    images = [four] + [second(four, d) for d in STEPS]
    far = along_z(jnp.concatenate([one, two[:rows]]), 2)
    part0, hi0, lo0, *start, thi, tlo = group_call(logit_scale, logit_bias, images[:1], [text_emb, other, one, two])
    part1, hi1, lo1, text_part, loss = group_call(logit_scale, logit_bias, images[1:], (thi, tlo), start)
    rest = swap(after(jnp.concatenate([one, two, far]), loss))
    ihi, ilo, far_part, *mid, loss = mid_call(logit_scale, logit_bias, (hi0, lo0, hi1, lo1), loss, far)
    *last, loss = far_call(logit_scale, logit_bias, ihi, ilo, loss, rest)
    pay, *four = last_call((ihi, ilo), mid, last, (part0, part1), text_part[rows : 2 * rows])
    loss = add_from(loss, lambda z, y, x, core: (z ^ 1, y, x, core))
    note = jnp.concatenate([jnp.broadcast_to(loss[:, at : at + 1], (8, text_emb.shape[1] // 2)) for at in (0, 127)], 1)
    got = swap(jnp.concatenate([pay, note]))
    note = note + got[8 * rows :]
    back = along_z(far_part + got[4 * rows : 7 * rows], -2)
    one_part = text_part[2 * rows : 4 * rows] + got[: 2 * rows]
    two_part = text_part[4 * rows :] + got[2 * rows : 4 * rows]
    own_part = text_part[:rows] + got[7 * rows : 8 * rows]
    four = [jnp.concatenate([block, note]) for block in four]
    got = [second(four[i + 1], -d) for i, d in enumerate(STEPS)]
    one_part = one_part + back[: 2 * rows]
    two_part = jnp.concatenate([two_part[:rows] + back[2 * rows :], two_part[rows:]])
    back = along_z(one_part, -1) + along_z(two_part, -2)
    four = sum_call([four[0]] + got)
    got = [first(four[i + 1], -d) for i, d in enumerate(STEPS)]
    total = (four[0] + got[2]) + (got[0] + got[1])
    text_unit_grad = own_part + back[:rows] + swap(back[rows:])
    image_unit_grad = total[:rows]
    loss = jnp.concatenate([total[rows:, :64], total[rows:, -64:]], 1)
    beside = along_z(loss, -2)
    loss = loss + send(loss, lambda z, y, x, core: (z + 4, y, x, core))
    loss = loss + beside + swap(beside)
    loss = ((loss[0, 0] + loss[0, 127]) / (rows * 2 * NX * NY * NZ)).reshape(1)

    image_unit, image_inv = normalize(image_emb)
    text_unit, text_inv = normalize(text_emb)
    image_grad = (
        image_unit_grad - image_unit * jnp.sum(image_unit * image_unit_grad, axis=1, keepdims=True)
    ) * image_inv
    text_grad = (
        text_unit_grad - text_unit * jnp.sum(text_unit * text_unit_grad, axis=1, keepdims=True)
    ) * text_inv
    return (loss, image_grad, text_grad)


def solution(mesh):
    return jax.shard_map(
        on_device,
        mesh=mesh,
        in_specs=(P(("img", "txt"), None), P(("img", "txt"), None), P(), P()),
        out_specs=(P(), P(("img", "txt"), None), P(("img", "txt"), None)),
        check_vma=False,
    )
```

```python
import functools
import itertools
import jax
import jax.numpy as jnp
from jax import lax
from jax.experimental import pallas as pl
from jax.experimental.pallas import tpu as pltpu
from jax.sharding import PartitionSpec as P

AXES = ("img", "txt")
NX, NY, NZ = 4, 4, 8


def place(z, y, x, core):
    return ((z // 2) * 2 + core) * 32 + (y * NX + x) * 2 + z % 2


def pairs(target):
    out = []
    for z, y, x, core in itertools.product(range(NZ), range(NY), range(NX), range(2)):
        tz, ty, tx, tc = target(z, y, x, core)
        out.append((place(z, y, x, core), place(tz % NZ, ty % NY, tx % NX, tc)))
    return out


def send(value, target):
    return lax.ppermute(value, AXES, pairs(target))


def swap(value):
    return send(value, lambda z, y, x, core: (z, y, x, 1 - core))


def first(value, d):
    return send(value, lambda z, y, x, core: (z, y, x + d, core) if core == 0 else (z, y + d, x, core))


def second(value, d):
    return send(value, lambda z, y, x, core: (z, y + d, x, core) if core == 0 else (z, y, x + d, core))


def along_z(value, d):
    return send(value, lambda z, y, x, core: (z + d if core == 0 else z - d, y, x, core))


STEPS = (1, 3, 2)

def add_from(value, target):
    return value + send(value, target)


def after(values, *others):
    return lax.optimization_barrier((values, others))[0]


NT = (((1,), (1,)), ((), ()))
TN = (((0,), (0,)), ((), ()))
NN = (((1,), (0,)), ((), ()))
VMEM = pl.BlockSpec(memory_space=pltpu.VMEM)
SMEM = pl.BlockSpec(memory_space=pltpu.SMEM)
GRANT = pltpu.CompilerParams(vmem_limit_bytes=40 << 20)


def f32(*shape):
    return jax.ShapeDtypeStruct(shape, jnp.float32)


def b16(*shape):
    return jax.ShapeDtypeStruct(shape, jnp.bfloat16)


def halves(value):
    high = value.astype(jnp.bfloat16)
    return high, (value - high.astype(jnp.float32)).astype(jnp.bfloat16)


def dot3(a, b, dims):
    dot = functools.partial(lax.dot_general, dimension_numbers=dims, preferred_element_type=jnp.float32)
    return dot(a[0], b[0]) + (dot(a[0], b[1]) + dot(a[1], b[0]))


def unit_halves(refs, high, low):
    at = 0
    for ref in refs:
        rows = ref.shape[0]
        raw = ref[...]
        unit = raw * lax.rsqrt(jnp.sum(raw * raw, axis=1, keepdims=True) + 1e-06)
        high[at : at + rows, :], low[at : at + rows, :] = halves(unit)
        at += rows


def pair_terms(logits, own):
    if own:
        row = lax.broadcasted_iota(jnp.int32, logits.shape, 0)
        col = lax.broadcasted_iota(jnp.int32, logits.shape, 1)
        same = (row == col) & (row < own)
        logits = jnp.where(same, -logits, logits)
    small = jnp.exp(-jnp.abs(logits))
    loss = jnp.sum(jnp.maximum(logits, 0.0) + jnp.log1p(small))
    part = 1.0 / (1.0 + small)
    coef = jnp.where(logits >= 0, part, small * part)
    if own:
        coef = jnp.where(same, -coef, coef)
    return loss, coef


def two_parts(total):
    coarse = jnp.round(total * (1.0 / 128.0)) * 128.0
    fine = jnp.round((total - coarse) * 512.0) * (1.0 / 512.0)
    return jnp.where(lax.broadcasted_iota(jnp.int32, (8, 128), 1) < 64, coarse, fine)


def group_kernel(own, count, scale, bias, *refs):
    raws = refs[:count]
    if own:
        texts = refs[count : count + 4]
        image_part, ihi, ilo, text_part, loss, thi, tlo = refs[count + 4 :]
        unit_halves(texts, thi, tlo)
    else:
        thi, tlo, text_in, loss_in, image_part, ihi, ilo, text_part, loss = refs[count:]
    unit_halves(raws, ihi, ilo)
    images = ihi[...], ilo[...]
    texts = thi[...], tlo[...]
    logits = scale[0] * dot3(images, texts, NT) + bias[0]
    total, coef = pair_terms(logits, own)
    coef = halves(coef * scale[0])
    image_part[...] = dot3(coef, texts, NN)
    part = dot3(coef, images, TN)
    if own:
        text_part[...] = part
        loss[...] = jnp.full(loss.shape, total, jnp.float32)
    else:
        text_part[...] = text_in[...] + part
        loss[...] = loss_in[...] + total


def mid_kernel(scale, bias, h0, l0, h1, l1, loss_in, raw, ihi, ilo, part, chi, clo, thi, tlo, loss):
    rows = h0.shape[0]
    ihi[:rows, :], ilo[:rows, :] = h0[...], l0[...]
    ihi[rows:, :], ilo[rows:, :] = h1[...], l1[...]
    unit_halves((raw,), thi, tlo)
    images = ihi[...], ilo[...]
    logits = scale[0] * dot3(images, (thi[...], tlo[...]), NT) + bias[0]
    total, coef = pair_terms(logits, 0)
    loss[...] = loss_in[...] + total
    coef = halves(coef * scale[0])
    chi[...], clo[...] = coef
    part[...] = dot3(coef, images, TN)


def far_kernel(scale, bias, ihi, ilo, loss_in, raw, chi, clo, thi, tlo, loss):
    unit_halves((raw,), thi, tlo)
    logits = scale[0] * dot3((ihi[...], ilo[...]), (thi[...], tlo[...]), NT) + bias[0]
    total, coef = pair_terms(logits, 0)
    loss[...] = two_parts(loss_in[...] + total)
    chi[...], clo[...] = halves(coef * scale[0])


def last_kernel(ihi, ilo, mhi, mlo, uhi, ulo, chi, clo, thi, tlo, in0, in1, other, pay, *outs):
    coef = chi[...], clo[...]
    count = thi.shape[0]
    pay[:count, :] = dot3(coef, (ihi[...], ilo[...]), TN)
    pay[count:, :] = other[...]
    part = dot3((mhi[...], mlo[...]), (uhi[...], ulo[...]), NN) + dot3(coef, (thi[...], tlo[...]), NN)
    rows = in0.shape[0]
    outs[0][...] = in0[...] + part[:rows]
    for k, out in enumerate(outs[1:]):
        out[...] = in1[rows * k : rows * (k + 1), :] + part[rows * (k + 1) : rows * (k + 2)]


def sum_kernel(in0, in1, in2, in3, out0, out1, out2, out3):
    total = (in0[...] + in3[...]) + (in1[...] + in2[...])
    rows = (total.shape[0] - 8) // 4
    for k, out in enumerate((out0, out1, out2, out3)):
        out[:rows, :] = total[rows * k : rows * (k + 1)]
        out[rows:, :] = total[4 * rows :]


def cost(rows, cols, width, dots):
    return pl.CostEstimate(flops=6 * dots * rows * cols * width, bytes_accessed=4 * rows * width, transcendentals=0)


def group_call(scale, bias, raws, texts, start=None):
    width = raws[0].shape[1]
    rows = sum(raw.shape[0] for raw in raws)
    cols = sum(text.shape[0] for text in texts) if start is None else texts[0].shape[0]
    operands = [scale, bias, *raws, *texts, *(start or ())]
    shapes = [f32(rows, width), b16(rows, width), b16(rows, width), f32(cols, width), f32(8, 128)]
    if start is None:
        shapes += [b16(cols, width)] * 2
    return pl.pallas_call(
        functools.partial(group_kernel, texts[0].shape[0] if start is None else 0, len(raws)),
        out_shape=shapes,
        in_specs=[SMEM, SMEM] + [VMEM] * (len(operands) - 2),
        out_specs=[VMEM] * len(shapes),
        cost_estimate=cost(rows, cols, width, 3),
        compiler_params=GRANT,
    )(*operands)


def mid_call(scale, bias, images, loss, raw):
    count, width = raw.shape
    rows = images[0].shape[0] + images[2].shape[0]
    return pl.pallas_call(
        mid_kernel,
        out_shape=[b16(rows, width)] * 2
        + [f32(count, width)]
        + [b16(rows, count)] * 2
        + [b16(count, width)] * 2
        + [f32(8, 128)],
        in_specs=[SMEM, SMEM] + [VMEM] * 6,
        out_specs=[VMEM] * 8,
        cost_estimate=cost(rows, count, width, 2),
        compiler_params=GRANT,
    )(scale, bias, *images, loss, raw)


def far_call(scale, bias, ihi, ilo, loss, raw):
    count, width = raw.shape
    rows = ihi.shape[0]
    return pl.pallas_call(
        far_kernel,
        out_shape=[b16(rows, count)] * 2 + [b16(count, width)] * 2 + [f32(8, 128)],
        in_specs=[SMEM, SMEM] + [VMEM] * 4,
        out_specs=[VMEM] * 5,
        cost_estimate=cost(rows, count, width, 1),
        compiler_params=GRANT,
    )(scale, bias, ihi, ilo, loss, raw)


def last_call(images, mid, far, starts, other):
    rows, width = images[0].shape
    count = far[0].shape[1]
    return pl.pallas_call(
        last_kernel,
        out_shape=[f32(count + other.shape[0], width)] + [f32(rows // 4, width)] * 4,
        in_specs=[VMEM] * 13,
        out_specs=[VMEM] * 5,
        cost_estimate=cost(rows, count, width, 5),
        compiler_params=GRANT,
    )(*images, *mid, *far, *starts, other)


def sum_call(parts):
    rows, width = parts[0].shape
    return pl.pallas_call(
        sum_kernel,
        out_shape=[f32((rows - 8) // 4 + 8, width)] * 4,
        in_specs=[VMEM] * 4,
        out_specs=[VMEM] * 4,
        compiler_params=GRANT,
    )(*parts)


def normalize(embed):
    inverse = lax.rsqrt(jnp.sum(embed * embed, axis=1, keepdims=True) + 1e-06)
    return (embed * inverse, inverse)


def on_device(image_emb, text_emb, logit_scale, logit_bias):
    rows = image_emb.shape[0]
    other = swap(text_emb)
    four = [first(image_emb, d) for d in STEPS]
    pair = jnp.concatenate([text_emb, other])
    one = along_z(pair, 1)
    two = along_z(pair, 2)
    four = jnp.concatenate([image_emb] + four)
    images = [four] + [second(four, d) for d in STEPS]
    far = along_z(jnp.concatenate([one, two[:rows]]), 2)
    part0, hi0, lo0, *start, thi, tlo = group_call(logit_scale, logit_bias, images[:1], [text_emb, other, one, two])
    part1, hi1, lo1, text_part, loss = group_call(logit_scale, logit_bias, images[1:], (thi, tlo), start)
    rest = swap(after(jnp.concatenate([one, two, far]), loss))
    ihi, ilo, far_part, *mid, loss = mid_call(logit_scale, logit_bias, (hi0, lo0, hi1, lo1), loss, far)
    *last, loss = far_call(logit_scale, logit_bias, ihi, ilo, loss, rest)
    pay, *four = last_call((ihi, ilo), mid, last, (part0, part1), text_part[rows : 2 * rows])
    loss = add_from(loss, lambda z, y, x, core: (z ^ 1, y, x, core))
    note = jnp.concatenate([jnp.broadcast_to(loss[:, at : at + 1], (8, text_emb.shape[1] // 2)) for at in (0, 127)], 1)
    got = swap(jnp.concatenate([pay, note]))
    note = note + got[8 * rows :]
    back = along_z(far_part + got[4 * rows : 7 * rows], -2)
    one_part = text_part[2 * rows : 4 * rows] + got[: 2 * rows]
    two_part = text_part[4 * rows :] + got[2 * rows : 4 * rows]
    own_part = text_part[:rows] + got[7 * rows : 8 * rows]
    four = [jnp.concatenate([block, note]) for block in four]
    got = [second(four[i + 1], -d) for i, d in enumerate(STEPS)]
    one_part = one_part + back[: 2 * rows]
    two_part = jnp.concatenate([two_part[:rows] + back[2 * rows :], two_part[rows:]])
    back = along_z(one_part, -1) + along_z(two_part, -2)
    four = sum_call([four[0]] + got)
    got = [first(four[i + 1], -d) for i, d in enumerate(STEPS)]
    total = (four[0] + got[2]) + (got[0] + got[1])
    text_unit_grad = own_part + back[:rows] + swap(back[rows:])
    image_unit_grad = total[:rows]
    loss = jnp.concatenate([total[rows:, :64], total[rows:, -64:]], 1)
    beside = along_z(loss, -2)
    loss = loss + send(loss, lambda z, y, x, core: (z + 4, y, x, core))

    image_unit, image_inv = normalize(image_emb)
    text_unit, text_inv = normalize(text_emb)
    image_grad = (
        image_unit_grad - image_unit * jnp.sum(image_unit * image_unit_grad, axis=1, keepdims=True)
    ) * image_inv
    text_grad = (
        text_unit_grad - text_unit * jnp.sum(text_unit * text_unit_grad, axis=1, keepdims=True)
    ) * text_inv
    loss = loss + beside + swap(after(beside, (image_grad, text_grad)))
    return ((loss[:1, 0] + loss[:1, 127]) / (rows * 2 * NX * NY * NZ), image_grad, text_grad)


def solution(mesh):
    return jax.shard_map(
        on_device,
        mesh=mesh,
        in_specs=(P(("img", "txt"), None), P(("img", "txt"), None), P(), P()),
        out_specs=(P(), P(("img", "txt"), None), P(("img", "txt"), None)),
        check_vma=False,
    )
```

```python
import functools
import itertools
import jax
import jax.numpy as jnp
from jax import lax
from jax.experimental import pallas as pl
from jax.experimental.pallas import tpu as pltpu
from jax.sharding import PartitionSpec as P

AXES = ("img", "txt")
NX, NY, NZ = 4, 4, 8


def place(z, y, x, core):
    return ((z // 2) * 2 + core) * 32 + (y * NX + x) * 2 + z % 2


def pairs(target):
    out = []
    for z, y, x, core in itertools.product(range(NZ), range(NY), range(NX), range(2)):
        tz, ty, tx, tc = target(z, y, x, core)
        out.append((place(z, y, x, core), place(tz % NZ, ty % NY, tx % NX, tc)))
    return out


def send(value, target):
    return lax.ppermute(value, AXES, pairs(target))


def swap(value):
    return send(value, lambda z, y, x, core: (z, y, x, 1 - core))


def first(value, d):
    return send(value, lambda z, y, x, core: (z, y, x + d, core) if core == 0 else (z, y + d, x, core))


def second(value, d):
    return send(value, lambda z, y, x, core: (z, y + d, x, core) if core == 0 else (z, y, x + d, core))


def along_z(value, d):
    return send(value, lambda z, y, x, core: (z + d if core == 0 else z - d, y, x, core))


STEPS = (1, 3, 2)

def add_from(value, target):
    return value + send(value, target)


def after(values, *others):
    return lax.optimization_barrier((values, others))[0]


NT = (((1,), (1,)), ((), ()))
TN = (((0,), (0,)), ((), ()))
NN = (((1,), (0,)), ((), ()))
VMEM = pl.BlockSpec(memory_space=pltpu.VMEM)
SMEM = pl.BlockSpec(memory_space=pltpu.SMEM)
GRANT = pltpu.CompilerParams(vmem_limit_bytes=40 << 20)


def f32(*shape):
    return jax.ShapeDtypeStruct(shape, jnp.float32)


def b16(*shape):
    return jax.ShapeDtypeStruct(shape, jnp.bfloat16)


def halves(value):
    high = value.astype(jnp.bfloat16)
    return high, (value - high.astype(jnp.float32)).astype(jnp.bfloat16)


def dot3(a, b, dims):
    dot = functools.partial(lax.dot_general, dimension_numbers=dims, preferred_element_type=jnp.float32)
    return dot(a[0], b[0]) + (dot(a[0], b[1]) + dot(a[1], b[0]))


def unit_halves(refs, high, low):
    at = 0
    for ref in refs:
        rows = ref.shape[0]
        raw = ref[...]
        unit = raw * lax.rsqrt(jnp.sum(raw * raw, axis=1, keepdims=True) + 1e-06)
        high[at : at + rows, :], low[at : at + rows, :] = halves(unit)
        at += rows


def pair_terms(logits, own):
    if own:
        row = lax.broadcasted_iota(jnp.int32, logits.shape, 0)
        col = lax.broadcasted_iota(jnp.int32, logits.shape, 1)
        same = (row == col) & (row < own)
        logits = jnp.where(same, -logits, logits)
    small = jnp.exp(-jnp.abs(logits))
    loss = jnp.sum(jnp.maximum(logits, 0.0) + jnp.log1p(small))
    part = 1.0 / (1.0 + small)
    coef = jnp.where(logits >= 0, part, small * part)
    if own:
        coef = jnp.where(same, -coef, coef)
    return loss, coef


def two_parts(total):
    coarse = jnp.round(total * (1.0 / 128.0)) * 128.0
    fine = jnp.round((total - coarse) * 512.0) * (1.0 / 512.0)
    return jnp.where(lax.broadcasted_iota(jnp.int32, (8, 128), 1) < 64, coarse, fine)


def group_kernel(own, count, scale, bias, *refs):
    raws = refs[:count]
    if own:
        texts = refs[count : count + 4]
        image_part, ihi, ilo, text_part, loss, thi, tlo = refs[count + 4 :]
        unit_halves(texts, thi, tlo)
    else:
        thi, tlo, text_in, loss_in, high, low, image_part, ihi, ilo, text_part, loss = refs[count:]
    before = ihi.shape[0] - image_part.shape[0]
    if before:
        ihi[:before, :], ilo[:before, :] = high[...], low[...]
    unit_halves(raws, ihi.at[before:, :], ilo.at[before:, :])
    images = ihi[before:, :], ilo[before:, :]
    texts = thi[...], tlo[...]
    logits = scale[0] * dot3(images, texts, NT) + bias[0]
    total, coef = pair_terms(logits, own)
    coef = halves(coef * scale[0])
    image_part[...] = dot3(coef, texts, NN)
    part = dot3(coef, images, TN)
    if own:
        text_part[...] = part
        loss[...] = jnp.full(loss.shape, total, jnp.float32)
    else:
        text_part[...] = text_in[...] + part
        loss[...] = loss_in[...] + total


def far_kernel(final, scale, bias, ihi, ilo, loss_in, raw, chi, clo, thi, tlo, loss):
    unit_halves((raw,), thi, tlo)
    logits = scale[0] * dot3((ihi[...], ilo[...]), (thi[...], tlo[...]), NT) + bias[0]
    total, coef = pair_terms(logits, 0)
    total = loss_in[...] + total
    loss[...] = two_parts(total) if final else total
    chi[...], clo[...] = halves(coef * scale[0])


def text_kernel(ihi, ilo, chi, clo, *refs):
    out = refs[-1]
    count = chi.shape[1]
    out[:count, :] = dot3((chi[...], clo[...]), (ihi[...], ilo[...]), TN)
    if len(refs) > 1:
        out[count:, :] = refs[0][...]


def last_kernel(mhi, mlo, uhi, ulo, chi, clo, thi, tlo, in0, in1, *outs):
    part = dot3((mhi[...], mlo[...]), (uhi[...], ulo[...]), NN)
    part = part + dot3((chi[...], clo[...]), (thi[...], tlo[...]), NN)
    rows = in0.shape[0]
    outs[0][...] = in0[...] + part[:rows]
    for k, out in enumerate(outs[1:]):
        out[...] = in1[rows * k : rows * (k + 1), :] + part[rows * (k + 1) : rows * (k + 2)]


def sum_kernel(in0, in1, in2, in3, out0, out1, out2, out3):
    total = (in0[...] + in3[...]) + (in1[...] + in2[...])
    rows = (total.shape[0] - 8) // 4
    for k, out in enumerate((out0, out1, out2, out3)):
        out[:rows, :] = total[rows * k : rows * (k + 1)]
        out[rows:, :] = total[4 * rows :]


def cost(rows, cols, width, dots):
    return pl.CostEstimate(flops=6 * dots * rows * cols * width, bytes_accessed=4 * rows * width, transcendentals=0)


def group_call(scale, bias, raws, texts, start=None):
    width = raws[0].shape[1]
    rows = sum(raw.shape[0] for raw in raws)
    cols = sum(text.shape[0] for text in texts) if start is None else texts[0].shape[0]
    operands = [scale, bias, *raws, *texts, *(start or ())]
    held = rows + (start[2].shape[0] if start else 0)
    shapes = [f32(rows, width), b16(held, width), b16(held, width), f32(cols, width), f32(8, 128)]
    if start is None:
        shapes += [b16(cols, width)] * 2
    return pl.pallas_call(
        functools.partial(group_kernel, texts[0].shape[0] if start is None else 0, len(raws)),
        out_shape=shapes,
        in_specs=[SMEM, SMEM] + [VMEM] * (len(operands) - 2),
        out_specs=[VMEM] * len(shapes),
        cost_estimate=cost(rows, cols, width, 3),
        compiler_params=GRANT,
    )(*operands)


def far_call(scale, bias, images, loss, raw, final):
    count, width = raw.shape
    rows = images[0].shape[0]
    return pl.pallas_call(
        functools.partial(far_kernel, final),
        out_shape=[b16(rows, count)] * 2 + [b16(count, width)] * 2 + [f32(8, 128)],
        in_specs=[SMEM, SMEM] + [VMEM] * 4,
        out_specs=[VMEM] * 5,
        cost_estimate=cost(rows, count, width, 1),
        compiler_params=GRANT,
    )(scale, bias, *images, loss, raw)


def text_call(images, coef, *more):
    rows, width = images[0].shape
    count = coef[0].shape[1]
    return pl.pallas_call(
        text_kernel,
        out_shape=f32(count + sum(block.shape[0] for block in more), width),
        in_specs=[VMEM] * (4 + len(more)),
        out_specs=VMEM,
        cost_estimate=cost(rows, count, width, 1),
        compiler_params=GRANT,
    )(*images, *coef, *more)


def last_call(mid, far, starts):
    rows = mid[0].shape[0]
    count, width = far[2].shape
    return pl.pallas_call(
        last_kernel,
        out_shape=[f32(rows // 4, width)] * 4,
        in_specs=[VMEM] * 10,
        out_specs=[VMEM] * 4,
        cost_estimate=cost(rows, count, width, 3),
        compiler_params=GRANT,
    )(*mid, *far, *starts)


def sum_call(parts):
    rows, width = parts[0].shape
    return pl.pallas_call(
        sum_kernel,
        out_shape=[f32((rows - 8) // 4 + 8, width)] * 4,
        in_specs=[VMEM] * 4,
        out_specs=[VMEM] * 4,
        compiler_params=GRANT,
    )(*parts)


def normalize(embed):
    inverse = lax.rsqrt(jnp.sum(embed * embed, axis=1, keepdims=True) + 1e-06)
    return (embed * inverse, inverse)


def on_device(image_emb, text_emb, logit_scale, logit_bias):
    rows = image_emb.shape[0]
    other = swap(text_emb)
    four = [first(image_emb, d) for d in STEPS]
    pair = jnp.concatenate([text_emb, other])
    one = along_z(pair, 1)
    two = along_z(pair, 2)
    four = jnp.concatenate([image_emb] + four)
    images = [four] + [second(four, d) for d in STEPS]
    far = along_z(jnp.concatenate([one, two[:rows]]), 2)
    part0, hi0, lo0, *start, thi, tlo = group_call(logit_scale, logit_bias, images[:1], [text_emb, other, one, two])
    part1, ihi, ilo, text_part, loss = group_call(logit_scale, logit_bias, images[1:], (thi, tlo), (*start, hi0, lo0))
    rest = swap(after(jnp.concatenate([one, two, far]), loss))
    images = ihi, ilo
    *mid, loss = far_call(logit_scale, logit_bias, images, loss, far, False)
    *last, loss = far_call(logit_scale, logit_bias, images, loss, rest, True)
    loss = add_from(loss, lambda z, y, x, core: (z ^ 1, y, x, core))
    pay = text_call(images, last[:2], text_part[rows : 2 * rows])
    four = last_call(mid, after(last, pay), (part0, part1))
    got = swap(pay)
    loss = after(loss, four)
    loss = loss + swap(loss)
    note = jnp.concatenate([jnp.broadcast_to(loss[:, at : at + 1], (8, text_emb.shape[1] // 2)) for at in (0, 127)], 1)
    note = after(note, got)
    far_part = text_call(images, after(mid[:2], four))
    back = along_z(far_part + got[4 * rows : 7 * rows], -2)
    one_part = text_part[2 * rows : 4 * rows] + got[: 2 * rows]
    two_part = text_part[4 * rows :] + got[2 * rows : 4 * rows]
    own_part = text_part[:rows] + got[7 * rows : 8 * rows]
    four = [jnp.concatenate([block, note]) for block in four]
    got = [second(four[i + 1], -d) for i, d in enumerate(STEPS)]
    one_part = one_part + back[: 2 * rows]
    two_part = jnp.concatenate([two_part[:rows] + back[2 * rows :], two_part[rows:]])
    back = along_z(one_part, -1) + along_z(two_part, -2)
    four = sum_call([four[0]] + got)
    got = [first(four[i + 1], -d) for i, d in enumerate(STEPS)]
    total = (four[0] + got[2]) + (got[0] + got[1])
    text_unit_grad = own_part + back[:rows] + swap(back[rows:])
    image_unit_grad = total[:rows]
    loss = jnp.concatenate([total[rows:, :64], total[rows:, -64:]], 1)
    beside = along_z(loss, -2)
    loss = loss + send(loss, lambda z, y, x, core: (z + 4, y, x, core))

    image_unit, image_inv = normalize(image_emb)
    text_unit, text_inv = normalize(text_emb)
    image_grad = (
        image_unit_grad - image_unit * jnp.sum(image_unit * image_unit_grad, axis=1, keepdims=True)
    ) * image_inv
    text_grad = (
        text_unit_grad - text_unit * jnp.sum(text_unit * text_unit_grad, axis=1, keepdims=True)
    ) * text_inv
    loss = loss + beside + swap(after(beside, (image_grad, text_grad)))
    return ((loss[:1, 0] + loss[:1, 127]) / (rows * 2 * NX * NY * NZ), image_grad, text_grad)


def solution(mesh):
    return jax.shard_map(
        on_device,
        mesh=mesh,
        in_specs=(P(("img", "txt"), None), P(("img", "txt"), None), P(), P()),
        out_specs=(P(), P(("img", "txt"), None), P(("img", "txt"), None)),
        check_vma=False,
    )
```

```python
import functools
import itertools
import jax
import jax.numpy as jnp
from jax import lax
from jax.experimental import pallas as pl
from jax.experimental.pallas import tpu as pltpu
from jax.sharding import PartitionSpec as P

AXES = ("img", "txt")
NX, NY, NZ = 4, 4, 8


def place(z, y, x, core):
    return ((z // 2) * 2 + core) * 32 + (y * NX + x) * 2 + z % 2


def pairs(target):
    out = []
    for z, y, x, core in itertools.product(range(NZ), range(NY), range(NX), range(2)):
        tz, ty, tx, tc = target(z, y, x, core)
        out.append((place(z, y, x, core), place(tz % NZ, ty % NY, tx % NX, tc)))
    return out


def send(value, target):
    return lax.ppermute(value, AXES, pairs(target))


def swap(value):
    return send(value, lambda z, y, x, core: (z, y, x, 1 - core))


def first(value, d):
    return send(value, lambda z, y, x, core: (z, y, x + d, core) if core == 0 else (z, y + d, x, core))


def second(value, d):
    return send(value, lambda z, y, x, core: (z, y + d, x, core) if core == 0 else (z, y, x + d, core))


def along_z(value, d):
    return send(value, lambda z, y, x, core: (z + d if core == 0 else z - d, y, x, core))


STEPS = (1, 3, 2)

def add_from(value, target):
    return value + send(value, target)


def after(values, *others):
    return lax.optimization_barrier((values, others))[0]


NT = (((1,), (1,)), ((), ()))
TN = (((0,), (0,)), ((), ()))
NN = (((1,), (0,)), ((), ()))
VMEM = pl.BlockSpec(memory_space=pltpu.VMEM)
SMEM = pl.BlockSpec(memory_space=pltpu.SMEM)
GRANT = pltpu.CompilerParams(vmem_limit_bytes=40 << 20)


def f32(*shape):
    return jax.ShapeDtypeStruct(shape, jnp.float32)


def b16(*shape):
    return jax.ShapeDtypeStruct(shape, jnp.bfloat16)


def halves(value):
    high = value.astype(jnp.bfloat16)
    return high, (value - high.astype(jnp.float32)).astype(jnp.bfloat16)


def dot3(a, b, dims):
    dot = functools.partial(lax.dot_general, dimension_numbers=dims, preferred_element_type=jnp.float32)
    return dot(a[0], b[0]) + (dot(a[0], b[1]) + dot(a[1], b[0]))


def unit_halves(refs, high, low):
    at = 0
    for ref in refs:
        rows = ref.shape[0]
        raw = ref[...]
        unit = raw * lax.rsqrt(jnp.sum(raw * raw, axis=1, keepdims=True) + 1e-06)
        high[at : at + rows, :], low[at : at + rows, :] = halves(unit)
        at += rows


def pair_terms(logits, own):
    if own:
        row = lax.broadcasted_iota(jnp.int32, logits.shape, 0)
        col = lax.broadcasted_iota(jnp.int32, logits.shape, 1)
        same = (row == col) & (row < own)
        logits = jnp.where(same, -logits, logits)
    small = jnp.exp(-jnp.abs(logits))
    loss = jnp.sum(jnp.maximum(logits, 0.0) + jnp.log1p(small))
    part = 1.0 / (1.0 + small)
    coef = jnp.where(logits >= 0, part, small * part)
    if own:
        coef = jnp.where(same, -coef, coef)
    return loss, coef


def two_parts(total):
    coarse = jnp.round(total * (1.0 / 128.0)) * 128.0
    fine = jnp.round((total - coarse) * 512.0) * (1.0 / 512.0)
    return jnp.where(lax.broadcasted_iota(jnp.int32, (8, 128), 1) < 64, coarse, fine)


def group_kernel(own, count, scale, bias, *refs):
    raws = refs[:count]
    if own:
        texts = refs[count : count + 4]
        image_part, ihi, ilo, text_part, loss, thi, tlo = refs[count + 4 :]
        unit_halves(texts, thi, tlo)
    else:
        thi, tlo, text_in, loss_in, high, low, image_part, ihi, ilo, text_part, loss = refs[count:]
    before = ihi.shape[0] - image_part.shape[0]
    if before:
        ihi[:before, :], ilo[:before, :] = high[...], low[...]
    unit_halves(raws, ihi.at[before:, :], ilo.at[before:, :])
    images = ihi[before:, :], ilo[before:, :]
    texts = thi[...], tlo[...]
    logits = scale[0] * dot3(images, texts, NT) + bias[0]
    total, coef = pair_terms(logits, own)
    coef = halves(coef * scale[0])
    image_part[...] = dot3(coef, texts, NN)
    part = dot3(coef, images, TN)
    if own:
        text_part[...] = part
        loss[...] = jnp.full(loss.shape, total, jnp.float32)
    else:
        text_part[...] = text_in[...] + part
        loss[...] = loss_in[...] + total


def far_kernel(final, scale, bias, ihi, ilo, loss_in, raw, chi, clo, thi, tlo, loss):
    unit_halves((raw,), thi, tlo)
    logits = scale[0] * dot3((ihi[...], ilo[...]), (thi[...], tlo[...]), NT) + bias[0]
    total, coef = pair_terms(logits, 0)
    total = loss_in[...] + total
    loss[...] = two_parts(total) if final else total
    chi[...], clo[...] = halves(coef * scale[0])


def text_kernel(ihi, ilo, chi, clo, *refs):
    out = refs[-1]
    count = chi.shape[1]
    out[:count, :] = dot3((chi[...], clo[...]), (ihi[...], ilo[...]), TN)
    if len(refs) > 1:
        out[count:, :] = refs[0][...]


def last_kernel(mhi, mlo, uhi, ulo, chi, clo, thi, tlo, in0, in1, *outs):
    part = dot3((mhi[...], mlo[...]), (uhi[...], ulo[...]), NN)
    part = part + dot3((chi[...], clo[...]), (thi[...], tlo[...]), NN)
    rows = in0.shape[0]
    outs[0][...] = in0[...] + part[:rows]
    for k, out in enumerate(outs[1:]):
        out[...] = in1[rows * k : rows * (k + 1), :] + part[rows * (k + 1) : rows * (k + 2)]


def sum_kernel(in0, in1, in2, in3, out0, out1, out2, out3):
    total = (in0[...] + in3[...]) + (in1[...] + in2[...])
    rows = (total.shape[0] - 8) // 4
    for k, out in enumerate((out0, out1, out2, out3)):
        out[:rows, :] = total[rows * k : rows * (k + 1)]
        out[rows:, :] = total[4 * rows :]


def cost(rows, cols, width, dots):
    return pl.CostEstimate(flops=6 * dots * rows * cols * width, bytes_accessed=4 * rows * width, transcendentals=0)


def group_call(scale, bias, raws, texts, start=None):
    width = raws[0].shape[1]
    rows = sum(raw.shape[0] for raw in raws)
    cols = sum(text.shape[0] for text in texts) if start is None else texts[0].shape[0]
    operands = [scale, bias, *raws, *texts, *(start or ())]
    held = rows + (start[2].shape[0] if start else 0)
    shapes = [f32(rows, width), b16(held, width), b16(held, width), f32(cols, width), f32(8, 128)]
    if start is None:
        shapes += [b16(cols, width)] * 2
    return pl.pallas_call(
        functools.partial(group_kernel, texts[0].shape[0] if start is None else 0, len(raws)),
        out_shape=shapes,
        in_specs=[SMEM, SMEM] + [VMEM] * (len(operands) - 2),
        out_specs=[VMEM] * len(shapes),
        cost_estimate=cost(rows, cols, width, 3),
        compiler_params=GRANT,
    )(*operands)


def far_call(scale, bias, images, loss, raw, final):
    count, width = raw.shape
    rows = images[0].shape[0]
    return pl.pallas_call(
        functools.partial(far_kernel, final),
        out_shape=[b16(rows, count)] * 2 + [b16(count, width)] * 2 + [f32(8, 128)],
        in_specs=[SMEM, SMEM] + [VMEM] * 4,
        out_specs=[VMEM] * 5,
        cost_estimate=cost(rows, count, width, 1),
        compiler_params=GRANT,
    )(scale, bias, *images, loss, raw)


def text_call(images, coef, *more):
    rows, width = images[0].shape
    count = coef[0].shape[1]
    return pl.pallas_call(
        text_kernel,
        out_shape=f32(count + sum(block.shape[0] for block in more), width),
        in_specs=[VMEM] * (4 + len(more)),
        out_specs=VMEM,
        cost_estimate=cost(rows, count, width, 1),
        compiler_params=GRANT,
    )(*images, *coef, *more)


def last_call(mid, far, starts):
    rows = mid[0].shape[0]
    count, width = far[2].shape
    return pl.pallas_call(
        last_kernel,
        out_shape=[f32(rows // 4, width)] * 4,
        in_specs=[VMEM] * 10,
        out_specs=[VMEM] * 4,
        cost_estimate=cost(rows, count, width, 3),
        compiler_params=GRANT,
    )(*mid, *far, *starts)


def sum_call(parts):
    rows, width = parts[0].shape
    return pl.pallas_call(
        sum_kernel,
        out_shape=[f32((rows - 8) // 4 + 8, width)] * 4,
        in_specs=[VMEM] * 4,
        out_specs=[VMEM] * 4,
        compiler_params=GRANT,
    )(*parts)


def normalize(embed):
    inverse = lax.rsqrt(jnp.sum(embed * embed, axis=1, keepdims=True) + 1e-06)
    return (embed * inverse, inverse)


def on_device(image_emb, text_emb, logit_scale, logit_bias):
    rows = image_emb.shape[0]
    other = swap(text_emb)
    four = [first(image_emb, d) for d in STEPS]
    pair = jnp.concatenate([text_emb, other])
    one = along_z(pair, 1)
    two = along_z(pair, 2)
    four = jnp.concatenate([image_emb] + four)
    images = [four] + [second(four, d) for d in STEPS]
    far = along_z(jnp.concatenate([one, two[:rows]]), 2)
    part0, hi0, lo0, *start, thi, tlo = group_call(logit_scale, logit_bias, images[:1], [text_emb, other, one, two])
    part1, ihi, ilo, text_part, loss = group_call(logit_scale, logit_bias, images[1:], (thi, tlo), (*start, hi0, lo0))
    rest = swap(after(jnp.concatenate([one, two, far]), loss))
    images = ihi, ilo
    *mid, loss = far_call(logit_scale, logit_bias, images, loss, far, False)
    *last, loss = far_call(logit_scale, logit_bias, images, loss, rest, True)
    loss = add_from(loss, lambda z, y, x, core: (z ^ 4, y, x, core))
    pay = text_call(images, last[:2], text_part[rows : 2 * rows])
    four = last_call(mid, after(last, pay), (part0, part1))
    got = swap(pay)
    loss = after(loss, four)
    loss = loss + swap(loss)
    note = jnp.concatenate([jnp.broadcast_to(loss[:, at : at + 1], (8, text_emb.shape[1] // 2)) for at in (0, 127)], 1)
    note = after(note, got)
    far_part = text_call(images, after(mid[:2], four))
    back = along_z(far_part + got[4 * rows : 7 * rows], -2)
    one_part = text_part[2 * rows : 4 * rows] + got[: 2 * rows]
    two_part = text_part[4 * rows :] + got[2 * rows : 4 * rows]
    own_part = text_part[:rows] + got[7 * rows : 8 * rows]
    four = [jnp.concatenate([block, note]) for block in four]
    got = [second(four[i + 1], -d) for i, d in enumerate(STEPS)]
    one_part = one_part + back[: 2 * rows]
    two_part = jnp.concatenate([two_part[:rows] + back[2 * rows :], two_part[rows:]])
    back = along_z(one_part, -1) + along_z(two_part, -2)
    four = sum_call([four[0]] + got)
    got = [first(four[i + 1], -d) for i, d in enumerate(STEPS)]
    total = (four[0] + got[2]) + (got[0] + got[1])
    text_unit_grad = own_part + back[:rows] + swap(back[rows:])
    image_unit_grad = total[:rows]
    loss = jnp.concatenate([total[rows:, :64], total[rows:, -64:]], 1)
    beside = along_z(loss, -1)
    loss = loss + along_z(loss, -2)

    image_unit, image_inv = normalize(image_emb)
    text_unit, text_inv = normalize(text_emb)
    image_grad = (
        image_unit_grad - image_unit * jnp.sum(image_unit * image_unit_grad, axis=1, keepdims=True)
    ) * image_inv
    text_grad = (
        text_unit_grad - text_unit * jnp.sum(text_unit * text_unit_grad, axis=1, keepdims=True)
    ) * text_inv
    loss = loss + beside + swap(after(beside, (image_grad, text_grad)))
    return ((loss[:1, 0] + loss[:1, 127]) / (rows * 2 * NX * NY * NZ), image_grad, text_grad)


def solution(mesh):
    return jax.shard_map(
        on_device,
        mesh=mesh,
        in_specs=(P(("img", "txt"), None), P(("img", "txt"), None), P(), P()),
        out_specs=(P(), P(("img", "txt"), None), P(("img", "txt"), None)),
        check_vma=False,
    )
```

```python
import functools
import itertools
import jax
import jax.numpy as jnp
from jax import lax
from jax.experimental import pallas as pl
from jax.experimental.pallas import tpu as pltpu
from jax.sharding import PartitionSpec as P

AXES = ("img", "txt")
NX, NY, NZ = 4, 4, 8


def place(z, y, x, core):
    return ((z // 2) * 2 + core) * 32 + (y * NX + x) * 2 + z % 2


def pairs(target):
    out = []
    for z, y, x, core in itertools.product(range(NZ), range(NY), range(NX), range(2)):
        tz, ty, tx, tc = target(z, y, x, core)
        out.append((place(z, y, x, core), place(tz % NZ, ty % NY, tx % NX, tc)))
    return out


def send(value, target):
    return lax.ppermute(value, AXES, pairs(target))


def swap(value):
    return send(value, lambda z, y, x, core: (z, y, x, 1 - core))


def first(value, d):
    return send(value, lambda z, y, x, core: (z, y, x + d, core) if core == 0 else (z, y + d, x, core))


def second(value, d):
    return send(value, lambda z, y, x, core: (z, y + d, x, core) if core == 0 else (z, y, x + d, core))


def along_z(value, d):
    return send(value, lambda z, y, x, core: (z + d if core == 0 else z - d, y, x, core))


STEPS = (1, 3, 2)

def add_from(value, target):
    return value + send(value, target)


def after(values, *others):
    return lax.optimization_barrier((values, others))[0]


NT = (((1,), (1,)), ((), ()))
TN = (((0,), (0,)), ((), ()))
NN = (((1,), (0,)), ((), ()))
VMEM = pl.BlockSpec(memory_space=pltpu.VMEM)
SMEM = pl.BlockSpec(memory_space=pltpu.SMEM)
GRANT = pltpu.CompilerParams(vmem_limit_bytes=40 << 20)


def f32(*shape):
    return jax.ShapeDtypeStruct(shape, jnp.float32)


def b16(*shape):
    return jax.ShapeDtypeStruct(shape, jnp.bfloat16)


def halves(value):
    high = value.astype(jnp.bfloat16)
    return high, (value - high.astype(jnp.float32)).astype(jnp.bfloat16)


def dot3(a, b, dims):
    dot = functools.partial(lax.dot_general, dimension_numbers=dims, preferred_element_type=jnp.float32)
    return dot(a[0], b[0]) + (dot(a[0], b[1]) + dot(a[1], b[0]))


def unit_halves(refs, high, low):
    at = 0
    for ref in refs:
        rows = ref.shape[0]
        raw = ref[...]
        unit = raw * lax.rsqrt(jnp.sum(raw * raw, axis=1, keepdims=True) + 1e-06)
        high[at : at + rows, :], low[at : at + rows, :] = halves(unit)
        at += rows


def pair_terms(logits, own):
    if own:
        row = lax.broadcasted_iota(jnp.int32, logits.shape, 0)
        col = lax.broadcasted_iota(jnp.int32, logits.shape, 1)
        same = (row == col) & (row < own)
        logits = jnp.where(same, -logits, logits)
    small = jnp.exp(-jnp.abs(logits))
    loss = jnp.sum(jnp.maximum(logits, 0.0) + jnp.log1p(small))
    part = 1.0 / (1.0 + small)
    coef = jnp.where(logits >= 0, part, small * part)
    if own:
        coef = jnp.where(same, -coef, coef)
    return loss, coef


def two_parts(total):
    coarse = jnp.round(total * (1.0 / 128.0)) * 128.0
    fine = jnp.round((total - coarse) * 512.0) * (1.0 / 512.0)
    return jnp.where(lax.broadcasted_iota(jnp.int32, (8, 128), 1) < 64, coarse, fine)


def group_kernel(own, count, scale, bias, *refs):
    raws = refs[:count]
    if own:
        texts = refs[count : count + 4]
        image_part, ihi, ilo, text_part, loss, thi, tlo = refs[count + 4 :]
        unit_halves(texts, thi, tlo)
    else:
        thi, tlo, text_in, loss_in, high, low, image_part, ihi, ilo, text_part, loss = refs[count:]
    before = ihi.shape[0] - image_part.shape[0]
    if before:
        ihi[:before, :], ilo[:before, :] = high[...], low[...]
    unit_halves(raws, ihi.at[before:, :], ilo.at[before:, :])
    images = ihi[before:, :], ilo[before:, :]
    texts = thi[...], tlo[...]
    logits = scale[0] * dot3(images, texts, NT) + bias[0]
    total, coef = pair_terms(logits, own)
    coef = halves(coef * scale[0])
    image_part[...] = dot3(coef, texts, NN)
    part = dot3(coef, images, TN)
    if own:
        text_part[...] = part
        loss[...] = jnp.full(loss.shape, total, jnp.float32)
    else:
        text_part[...] = text_in[...] + part
        loss[...] = loss_in[...] + total


def far_kernel(final, scale, bias, ihi, ilo, loss_in, raw, chi, clo, thi, tlo, loss):
    unit_halves((raw,), thi, tlo)
    logits = scale[0] * dot3((ihi[...], ilo[...]), (thi[...], tlo[...]), NT) + bias[0]
    total, coef = pair_terms(logits, 0)
    total = loss_in[...] + total
    loss[...] = two_parts(total) if final else total
    chi[...], clo[...] = halves(coef * scale[0])


def text_kernel(ihi, ilo, chi, clo, *refs):
    out = refs[-1]
    count = chi.shape[1]
    out[:count, :] = dot3((chi[...], clo[...]), (ihi[...], ilo[...]), TN)
    if len(refs) > 1:
        out[count:, :] = refs[0][...]


def last_kernel(mhi, mlo, uhi, ulo, chi, clo, thi, tlo, in0, in1, *outs):
    part = dot3((mhi[...], mlo[...]), (uhi[...], ulo[...]), NN)
    part = part + dot3((chi[...], clo[...]), (thi[...], tlo[...]), NN)
    rows = in0.shape[0]
    outs[0][...] = in0[...] + part[:rows]
    for k, out in enumerate(outs[1:]):
        out[...] = in1[rows * k : rows * (k + 1), :] + part[rows * (k + 1) : rows * (k + 2)]


def sum_kernel(in0, in1, in2, in3, out0, out1, out2, out3):
    total = (in0[...] + in3[...]) + (in1[...] + in2[...])
    rows = (total.shape[0] - 8) // 4
    for k, out in enumerate((out0, out1, out2, out3)):
        out[:rows, :] = total[rows * k : rows * (k + 1)]
        out[rows:, :] = total[4 * rows :]


def cost(rows, cols, width, dots):
    return pl.CostEstimate(flops=6 * dots * rows * cols * width, bytes_accessed=4 * rows * width, transcendentals=0)


def group_call(scale, bias, raws, texts, start=None):
    width = raws[0].shape[1]
    rows = sum(raw.shape[0] for raw in raws)
    cols = sum(text.shape[0] for text in texts) if start is None else texts[0].shape[0]
    operands = [scale, bias, *raws, *texts, *(start or ())]
    held = rows + (start[2].shape[0] if start else 0)
    shapes = [f32(rows, width), b16(held, width), b16(held, width), f32(cols, width), f32(8, 128)]
    if start is None:
        shapes += [b16(cols, width)] * 2
    return pl.pallas_call(
        functools.partial(group_kernel, texts[0].shape[0] if start is None else 0, len(raws)),
        out_shape=shapes,
        in_specs=[SMEM, SMEM] + [VMEM] * (len(operands) - 2),
        out_specs=[VMEM] * len(shapes),
        cost_estimate=cost(rows, cols, width, 3),
        compiler_params=GRANT,
    )(*operands)


def far_call(scale, bias, images, loss, raw, final):
    count, width = raw.shape
    rows = images[0].shape[0]
    return pl.pallas_call(
        functools.partial(far_kernel, final),
        out_shape=[b16(rows, count)] * 2 + [b16(count, width)] * 2 + [f32(8, 128)],
        in_specs=[SMEM, SMEM] + [VMEM] * 4,
        out_specs=[VMEM] * 5,
        cost_estimate=cost(rows, count, width, 1),
        compiler_params=GRANT,
    )(scale, bias, *images, loss, raw)


def text_call(images, coef, *more):
    rows, width = images[0].shape
    count = coef[0].shape[1]
    return pl.pallas_call(
        text_kernel,
        out_shape=f32(count + sum(block.shape[0] for block in more), width),
        in_specs=[VMEM] * (4 + len(more)),
        out_specs=VMEM,
        cost_estimate=cost(rows, count, width, 1),
        compiler_params=GRANT,
    )(*images, *coef, *more)


def last_call(mid, far, starts):
    rows = mid[0].shape[0]
    count, width = far[2].shape
    return pl.pallas_call(
        last_kernel,
        out_shape=[f32(rows // 4, width)] * 4,
        in_specs=[VMEM] * 10,
        out_specs=[VMEM] * 4,
        cost_estimate=cost(rows, count, width, 3),
        compiler_params=GRANT,
    )(*mid, *far, *starts)


def sum_call(parts):
    rows, width = parts[0].shape
    return pl.pallas_call(
        sum_kernel,
        out_shape=[f32((rows - 8) // 4 + 8, width)] * 4,
        in_specs=[VMEM] * 4,
        out_specs=[VMEM] * 4,
        compiler_params=GRANT,
    )(*parts)


def normalize(embed):
    inverse = lax.rsqrt(jnp.sum(embed * embed, axis=1, keepdims=True) + 1e-06)
    return (embed * inverse, inverse)


def on_device(image_emb, text_emb, logit_scale, logit_bias):
    rows = image_emb.shape[0]
    other = swap(text_emb)
    four = [first(image_emb, d) for d in STEPS]
    pair = jnp.concatenate([text_emb, other])
    one = along_z(pair, 1)
    two = along_z(pair, 2)
    four = jnp.concatenate([image_emb] + four)
    images = [four] + [second(four, d) for d in STEPS]
    far = along_z(jnp.concatenate([one, two[:rows]]), 2)
    part0, hi0, lo0, *start, thi, tlo = group_call(logit_scale, logit_bias, images[:1], [text_emb, other, one, two])
    part1, ihi, ilo, text_part, loss = group_call(logit_scale, logit_bias, images[1:], (thi, tlo), (*start, hi0, lo0))
    rest = swap(after(jnp.concatenate([one, two, far]), loss))
    images = ihi, ilo
    *mid, loss = far_call(logit_scale, logit_bias, images, loss, far, False)
    *last, loss = far_call(logit_scale, logit_bias, images, loss, rest, True)
    loss = add_from(loss, lambda z, y, x, core: (z ^ 1, y, x, core))
    pay = text_call(images, last[:2], text_part[rows : 2 * rows])
    four = last_call(mid, after(last, pay), (part0, part1))
    got = swap(pay)
    loss = after(loss, four)
    loss = loss + swap(loss)
    note = jnp.concatenate([jnp.broadcast_to(loss[:, at : at + 1], (8, text_emb.shape[1] // 2)) for at in (0, 127)], 1)
    note = after(note, got)
    far_part = text_call(images, after(mid[:2], four))
    back = along_z(far_part + got[4 * rows : 7 * rows], -2)
    one_part = text_part[2 * rows : 4 * rows] + got[: 2 * rows]
    two_part = text_part[4 * rows :] + got[2 * rows : 4 * rows]
    own_part = text_part[:rows] + got[7 * rows : 8 * rows]
    four = [jnp.concatenate([block, note]) for block in four]
    got = [second(four[i + 1], -d) for i, d in enumerate(STEPS)]
    one_part = one_part + back[: 2 * rows]
    two_part = jnp.concatenate([two_part[:rows] + back[2 * rows :], two_part[rows:]])
    back = along_z(one_part, -1) + along_z(two_part, -2)
    four = sum_call([four[0]] + got)
    got = [first(four[i + 1], -d) for i, d in enumerate(STEPS)]
    total = (four[0] + got[2]) + (got[0] + got[1])
    text_unit_grad = own_part + back[:rows] + swap(back[rows:])
    image_unit_grad = total[:rows]
    loss = jnp.concatenate([total[rows:, :64], total[rows:, -64:]], 1)
    beside = along_z(loss, -2)
    loss = loss + send(loss, lambda z, y, x, core: (z + 4, y, x, core))

    image_unit, image_inv = normalize(image_emb)
    text_unit, text_inv = normalize(text_emb)
    image_grad = (
        image_unit_grad - image_unit * jnp.sum(image_unit * image_unit_grad, axis=1, keepdims=True)
    ) * image_inv
    text_grad = (
        text_unit_grad - text_unit * jnp.sum(text_unit * text_unit_grad, axis=1, keepdims=True)
    ) * text_inv
    loss = loss + beside + swap(after(beside, text_grad))
    loss = after(loss, image_grad)
    return ((loss[:1, 0] + loss[:1, 127]) / (rows * 2 * NX * NY * NZ), image_grad, text_grad)


def solution(mesh):
    return jax.shard_map(
        on_device,
        mesh=mesh,
        in_specs=(P(("img", "txt"), None), P(("img", "txt"), None), P(), P()),
        out_specs=(P(), P(("img", "txt"), None), P(("img", "txt"), None)),
        check_vma=False,
    )
```
